32 devices in a mesh: head: 2 (over x), seq: 16 (over z, y, core).
Axes of the slice: x: 2, y: 2, z: 4, core: 2. Of those that a mesh axis runs over, the one named last changes fastest.
Arguments:
- activations: bfloat16 [2048, 4096], P('seq'), may hold values from -6 to 6
- w_query: bfloat16 [3, 4096, 2048], P(None, 'seq', 'head'), may hold values from -32 to 32
- w_keyval: bfloat16 [3, 4096, 1024], P(None, 'seq'), may hold values from -32 to 32
- q_gain: float32 [3, 2048], P(None, 'head'), may hold values from 0.1 to 1.9
- k_gain: float32 [3, 512], replicated, may hold values from 0.1 to 1.9
- stream_ids: int32 [2048], P('seq'), may hold values from 0 to 2
- local_times: int32 [2048], P('seq'), may hold values from 0 to 31
- block_map: int32 [32], replicated, may hold values from 0 to 31, each once
Outputs:
- attended: bfloat16 [2048, 2048], P('seq', 'head')
The draws below stay inside these ranges and needn't reach their ends.
Inputs may be any that keep to these rules, and one draw needn't show every extreme that they name: `block_map`: a permutation of the block indices.
All inputs are finite; a program needn't handle non-finite values.
Results may differ from the reference program's by a relative error of at most 0.012.
The reference program's roundings to bfloat16 on the way (of `values`, `q_normed` and `k_normed`) count: a program that leaves them out, or rounds other values in their place, can miss the bound.
Values may be sent and summed in bfloat16 or wider, within the bound.
No kernel may reach another device: no remote copies, remote signals or barrier semaphores. Data moves between devices by JAX's collectives and lax.ppermute only.
A program may use at most 128 MiB of HBM per device.

```python
import math
import jax
import jax.numpy as jnp
from jax import lax

D = 4096
HEADS = 16
KV_HEADS = 4
HEAD_DIM = 128
STREAMS = 3
FRAMES = 32
ROWS_DEV = 128
TOKENS = 2048
BLOCK_ROWS = 64
BLOCKS = 32


def draw_activations(key, part):
    values = jax.random.normal(jax.random.fold_in(key, 301), (TOKENS, D), jnp.float32)
    return jnp.clip(values, -6.0, 6.0).astype(jnp.bfloat16)


def draw_w_query(key, part):
    base_draw = jnp.clip(jax.random.normal(jax.random.fold_in(key, 101), (STREAMS, D, HEADS * HEAD_DIM), jnp.float32), -6.0, 6.0) / jnp.sqrt(jnp.float32(D))
    return base_draw.astype(jnp.bfloat16)


def draw_w_keyval(key, part):
    base_draw = jnp.clip(jax.random.normal(jax.random.fold_in(key, 201), (STREAMS, D, 2 * KV_HEADS * HEAD_DIM), jnp.float32), -6.0, 6.0) / jnp.sqrt(jnp.float32(D))
    return base_draw.astype(jnp.bfloat16)


def draw_q_gain(key, part):
    values = 1.0 + 0.18 * jnp.clip(jax.random.normal(jax.random.fold_in(key, 401), (STREAMS, HEADS * HEAD_DIM), jnp.float32), -5.0, 5.0)
    return values


def draw_k_gain(key, part):
    values = 1.0 + 0.18 * jnp.clip(jax.random.normal(jax.random.fold_in(key, 501), (STREAMS, KV_HEADS * HEAD_DIM), jnp.float32), -5.0, 5.0)
    return values


def set_ends(values, key, smallest, largest):
    spot = [jax.random.randint(jax.random.fold_in(key, axis), (), 0, length) for axis, length in enumerate(values.shape)]
    main_axis = values.shape.index(max(values.shape))
    next_to = spot[:main_axis] + [(spot[main_axis] + 1) % values.shape[main_axis]] + spot[main_axis + 1:]
    return values.at[tuple(spot)].set(smallest).at[tuple(next_to)].set(largest)


def setup_inputs(seed: int = 0) -> dict:
    keys = jax.random.split(jax.random.key(seed), 9)
    activations = draw_activations(jax.random.fold_in(keys[8], 71), 0)
    w_query = draw_w_query(jax.random.fold_in(keys[8], 71), 0)
    w_keyval = draw_w_keyval(jax.random.fold_in(keys[8], 71), 0)
    q_gain = draw_q_gain(jax.random.fold_in(keys[8], 71), 0)
    k_gain = draw_k_gain(jax.random.fold_in(keys[8], 71), 0)
    stream_ids = set_ends(jax.random.randint(keys[5], (TOKENS,), 0, STREAMS), jax.random.fold_in(keys[5], 1), 0, STREAMS - 1).astype(jnp.int32)
    local_times = set_ends(jax.random.randint(keys[6], (TOKENS,), 0, FRAMES), jax.random.fold_in(keys[6], 1), 0, FRAMES - 1).astype(jnp.int32)
    block_map = jax.random.permutation(keys[7], BLOCKS).astype(jnp.int32)
    return dict(activations=activations, w_query=w_query, w_keyval=w_keyval, q_gain=q_gain, k_gain=k_gain, stream_ids=stream_ids, local_times=local_times, block_map=block_map)


epsilon = 1e-06

def reference(activations, w_query, w_keyval, q_gain, k_gain, stream_ids, local_times, block_map):
    group_size = HEADS // KV_HEADS
    stream_match = stream_ids[:, None] == jnp.arange(STREAMS, dtype=jnp.int32)[None, :]
    queries = jnp.zeros((TOKENS, HEADS * HEAD_DIM), jnp.float32)
    key_value = jnp.zeros((TOKENS, KV_HEADS * 2 * HEAD_DIM), jnp.float32)
    for stream in range(STREAMS):
        chosen = stream_match[:, stream:stream + 1]
        queries = queries + jnp.where(chosen, jnp.dot(activations, w_query[stream], preferred_element_type=jnp.float32), jnp.float32(0.0))
        key_value = key_value + jnp.where(chosen, jnp.dot(activations, w_keyval[stream], preferred_element_type=jnp.float32), jnp.float32(0.0))
    key_value = key_value.reshape(TOKENS, KV_HEADS, 2, HEAD_DIM)
    keys_raw = key_value[:, :, 0].reshape(TOKENS, KV_HEADS * HEAD_DIM)
    values = key_value[:, :, 1].astype(jnp.bfloat16)
    onehot = stream_match.astype(jnp.float32)
    q_scale = jnp.dot(onehot, q_gain, precision=lax.Precision.HIGHEST)
    k_scale = jnp.dot(onehot, k_gain, precision=lax.Precision.HIGHEST)
    q_normed = (queries * lax.rsqrt(lax.optimization_barrier(jnp.mean(queries * queries, axis=1)) + epsilon)[:, None] * q_scale).astype(jnp.bfloat16)
    q_normed = q_normed.reshape(TOKENS, KV_HEADS, group_size, HEAD_DIM)
    k_normed = (keys_raw * lax.rsqrt(lax.optimization_barrier(jnp.mean(keys_raw * keys_raw, axis=1)) + epsilon)[:, None] * k_scale).astype(jnp.bfloat16)
    k_normed = k_normed.reshape(TOKENS, KV_HEADS, HEAD_DIM)
    time_pos = block_map[jnp.arange(TOKENS, dtype=jnp.int32) // BLOCK_ROWS] * FRAMES + local_times
    key_float = k_normed.astype(jnp.float32)
    value_float = values.astype(jnp.float32)
    score_scale = 1.0 / math.sqrt(HEAD_DIM)
    block_count = TOKENS // ROWS_DEV

    def attend(inputs):
        query_block, query_times = inputs
        scores = jnp.einsum('rkgd,nkd->rkgn', query_block.astype(jnp.float32), key_float) * score_scale
        visible = time_pos[None, None, None, :] <= query_times[:, None, None, None]
        row_peak = lax.optimization_barrier(jnp.max(jnp.where(visible, scores, -1e+30), axis=3, keepdims=True))
        exp_terms = jnp.where(visible, jnp.exp(scores - row_peak), jnp.float32(0.0))
        row_total = lax.optimization_barrier(jnp.sum(exp_terms, axis=3))
        mixed_out = jnp.einsum('rkgn,nkd->rkgd', exp_terms.astype(jnp.bfloat16).astype(jnp.float32), value_float)
        return (mixed_out / row_total[..., None]).reshape(ROWS_DEV, HEADS * HEAD_DIM).astype(jnp.bfloat16)
    result = lax.map(attend, (q_normed.reshape(block_count, ROWS_DEV, KV_HEADS, group_size, HEAD_DIM), time_pos.reshape(block_count, ROWS_DEV)))
    return result.reshape(TOKENS, HEADS * HEAD_DIM)
```

```python
import functools
import math

import jax
import jax.numpy as jnp
from jax import lax
from jax.experimental import pallas as pl
from jax.experimental.pallas import tpu as pltpu
from jax.sharding import PartitionSpec as P

HEADS = 16
KV_HEADS = 4
HEAD_DIM = 128
STREAMS = 3
FRAMES = 32
NEAR = 4
INFO = 8

epsilon = 1e-06
MIB = 1024 * 1024

VMEM = pl.BlockSpec(memory_space=pltpu.VMEM)
SMEM = pl.BlockSpec(memory_space=pltpu.SMEM)


def params(mib):
    return pltpu.CompilerParams(vmem_limit_bytes=mib * MIB)


def swap(x, mask):
    size = lax.axis_size("seq")
    return lax.ppermute(x, "seq", [(i, i ^ mask) for i in range(size)])


def head_sum(x):
    size = lax.axis_size("head")
    step = 1
    while step < size:
        x = x + lax.ppermute(x, "head", [(i, i ^ step) for i in range(size)])
        step *= 2
    return x


def to_row(column):
    return jnp.broadcast_to(column, (column.shape[0], 128)).T[:8]


def to_column(row):
    return jnp.broadcast_to(row, (128, row.shape[1])).T[:, :1]


def by_stream(ids, gain_ref, first, width):
    gain = jnp.zeros((ids.shape[0], width), jnp.float32)
    for s in range(STREAMS):
        gain = jnp.where(ids == s, gain_ref[s:s + 1, first:first + width], gain)
    return gain


def pack_kernel(far, me_ref, x_ref, info_ref, *out_refs):
    rows = x_ref.shape[0]
    width = x_ref.shape[1] // far
    me = me_ref[0] // NEAR
    info = info_ref[...].astype(jnp.bfloat16)
    for k in range(far):
        first = pl.multiple_of((me ^ k) * width, 128)
        out_refs[k][:rows] = x_ref[:, pl.ds(first, width)]
        out_refs[k][rows:, :rows] = info


def pack(x, info, me, far):
    rows, width = x.shape
    return pl.pallas_call(
        functools.partial(pack_kernel, far),
        out_shape=[jax.ShapeDtypeStruct((rows + INFO, width // far), x.dtype)] * far,
        in_specs=[SMEM, VMEM, VMEM],
        out_specs=[VMEM] * far,
        compiler_params=params(16),
        cost_estimate=pl.CostEstimate(flops=0, bytes_accessed=4 * rows * width, transcendentals=0),
        name="pack",
    )(me, x, info)


def project_kernel(far, rows, w_ref, *refs):
    x_refs, out_refs = refs[:far], refs[far:]
    x = jnp.concatenate([ref[:rows] for ref in x_refs], axis=0)
    ids = jnp.concatenate(
        [to_column(ref[rows:rows + 1, :rows].astype(jnp.float32)) for ref in x_refs], axis=0
    )
    total = None
    for s in range(STREAMS):
        chosen = jnp.where(ids == s, x, jnp.zeros_like(x))
        term = jnp.dot(chosen, w_ref[s], preferred_element_type=jnp.float32)
        total = term if total is None else total + term
    out_refs[0][...] = total[:rows]
    for k in range(1, far):
        out_refs[k][...] = total[k * rows:(k + 1) * rows].astype(jnp.bfloat16)


def project(x_parts, w):
    far = len(x_parts)
    padded, width = x_parts[0].shape
    rows = padded - INFO
    streams, depth, columns = w.shape
    tile = min(256, columns)
    shapes = [jax.ShapeDtypeStruct((rows, columns), jnp.float32)]
    shapes += [jax.ShapeDtypeStruct((rows, columns), jnp.bfloat16)] * (far - 1)
    return pl.pallas_call(
        functools.partial(project_kernel, far, rows),
        grid=(columns // tile,),
        out_shape=shapes,
        in_specs=[pl.BlockSpec((streams, depth, tile), lambda i: (0, 0, i))]
        + [pl.BlockSpec((padded, width), lambda i: (0, 0))] * far,
        out_specs=[pl.BlockSpec((rows, tile), lambda i: (0, i))] * far,
        compiler_params=params(24),
        cost_estimate=pl.CostEstimate(
            flops=2 * far * rows * width * streams * columns,
            bytes_accessed=2 * (far * rows * (width + columns) + streams * depth * columns),
            transcendentals=0,
        ),
        name="project",
    )(w, *x_parts)


def reduce_kernel(count, square_columns, *refs):
    part_refs, total_refs, square_ref = refs[:count], refs[count:-1], refs[-1]
    each = count // len(total_refs)
    squares = None
    for t, total_ref in enumerate(total_refs):
        total = part_refs[t * each][...]
        for ref in part_refs[t * each + 1:(t + 1) * each]:
            total = total + ref[...].astype(jnp.float32)
        total_ref[...] = total
        for first in range(0, total.shape[1], 2 * HEAD_DIM):
            block = total[:, first:first + square_columns]
            term = jnp.sum(block * block, axis=1, keepdims=True)
            squares = term if squares is None else squares + term
    square_ref[...] = to_row(squares)


def reduce(part_lists, square_columns):
    parts = [part for parts in part_lists for part in parts]
    shape = part_lists[0][0].shape
    return pl.pallas_call(
        functools.partial(reduce_kernel, len(parts), square_columns),
        out_shape=[jax.ShapeDtypeStruct(shape, jnp.float32)] * len(part_lists)
        + [jax.ShapeDtypeStruct((8, shape[0]), jnp.float32)],
        in_specs=[VMEM] * len(parts),
        out_specs=[VMEM] * (len(part_lists) + 1),
        compiler_params=params(16),
        cost_estimate=pl.CostEstimate(
            flops=2 * len(parts) * shape[0] * shape[1],
            bytes_accessed=3 * len(parts) * shape[0] * shape[1],
            transcendentals=0,
        ),
        name="reduce",
    )(*parts)


def normalize_kernel(total_ref, square_ref, gain_ref, x_ref, out_ref):
    rows = total_ref.shape[0]
    ids = to_column(x_ref[rows:rows + 1, :rows].astype(jnp.float32))
    scale = to_column(lax.rsqrt(square_ref[:1] / (KV_HEADS * HEAD_DIM) + epsilon))
    for g in range(gain_ref.shape[1] // HEAD_DIM):
        first = 2 * g * HEAD_DIM
        gain = by_stream(ids, gain_ref, g * HEAD_DIM, HEAD_DIM)
        key = total_ref[:, first:first + HEAD_DIM] * scale * gain
        out_ref[:, first:first + HEAD_DIM] = key.astype(jnp.bfloat16)
        value = total_ref[:, first + HEAD_DIM:first + 2 * HEAD_DIM]
        out_ref[:, first + HEAD_DIM:first + 2 * HEAD_DIM] = value.astype(jnp.bfloat16)


def normalize(total, squares, gain, x_own):
    return pl.pallas_call(
        normalize_kernel,
        out_shape=jax.ShapeDtypeStruct(total.shape, jnp.bfloat16),
        in_specs=[VMEM] * 4,
        out_specs=VMEM,
        compiler_params=params(16),
        cost_estimate=pl.CostEstimate(
            flops=4 * total.size, bytes_accessed=6 * total.size, transcendentals=0
        ),
        name="normalize",
    )(total, squares, gain, x_own)


def attend_kernel(kv_local, per_group, q_count, far, me_ref, map_ref, x_ref, square_ref, gain_ref,
                  *refs):
    q_refs, kv_refs, out_ref = refs[:q_count], refs[q_count:q_count + NEAR], refs[-1]
    rows, columns = q_refs[0].shape
    keys = far * rows
    kv_columns = kv_refs[0].shape[1]
    score_scale = 1.0 / math.sqrt(HEAD_DIM)
    me = me_ref[0]
    first_half = lax.broadcasted_iota(jnp.int32, (1, rows), 1) < rows // 2
    ids = to_column(x_ref[rows:rows + 1, :rows].astype(jnp.float32))
    q_scale = to_column(lax.rsqrt(square_ref[:1] / (HEADS * HEAD_DIM) + epsilon))

    key_times = []
    for j in range(NEAR):
        pieces = []
        for k in range(far):
            owner = me ^ (k * NEAR + j)
            row, lane = divmod(k * rows, kv_columns)
            local = kv_refs[j][keys + row:keys + row + 1, lane:lane + rows].astype(jnp.float32)
            block = jnp.where(first_half, map_ref[2 * owner], map_ref[2 * owner + 1])
            pieces.append((block * FRAMES).astype(jnp.float32) + local)
        key_times.append(jnp.concatenate(pieces, axis=1))
    query_times = to_column(key_times[0][:, :rows])

    for g in range(kv_local):
        for h in range(per_group):
            head = g * per_group + h
            chunk, first = divmod(head * HEAD_DIM, columns)
            gain = by_stream(ids, gain_ref, head * HEAD_DIM, HEAD_DIM)
            q = (q_refs[chunk][:, first:first + HEAD_DIM] * q_scale * gain).astype(jnp.bfloat16)
            scores = []
            for j in range(NEAR):
                key = kv_refs[j][:keys, 2 * g * HEAD_DIM:(2 * g + 1) * HEAD_DIM]
                score = lax.dot_general(
                    q, key, (((1,), (1,)), ((), ())), preferred_element_type=jnp.float32
                )
                scores.append(jnp.where(key_times[j] <= query_times, score * score_scale, -1e30))
            peak = functools.reduce(
                jnp.maximum, [jnp.max(s, axis=1, keepdims=True) for s in scores]
            )
            total = jnp.zeros((rows, 1), jnp.float32)
            mixed = jnp.zeros((rows, HEAD_DIM), jnp.float32)
            for j in range(NEAR):
                value = kv_refs[j][:keys, (2 * g + 1) * HEAD_DIM:(2 * g + 2) * HEAD_DIM]
                terms = jnp.exp(scores[j] - peak)
                total = total + jnp.sum(terms, axis=1, keepdims=True)
                mixed = mixed + jnp.dot(
                    terms.astype(jnp.bfloat16), value, preferred_element_type=jnp.float32
                )
            out = (mixed / total).astype(out_ref.dtype)
            out_ref[:, head * HEAD_DIM:(head + 1) * HEAD_DIM] = out


def attend(me, block_map, x_own, squares, q_gain, q_parts, kv_parts, far, kv_local, per_group):
    rows, columns = q_parts[0].shape
    keys = NEAR * far * rows
    count = rows * kv_local * per_group * keys
    return pl.pallas_call(
        functools.partial(attend_kernel, kv_local, per_group, len(q_parts), far),
        out_shape=jax.ShapeDtypeStruct((rows, columns * len(q_parts)), jnp.bfloat16),
        in_specs=[SMEM, SMEM] + [VMEM] * (3 + len(q_parts) + NEAR),
        out_specs=VMEM,
        compiler_params=params(40),
        cost_estimate=pl.CostEstimate(
            flops=4 * count * HEAD_DIM,
            bytes_accessed=4 * keys * kv_local * HEAD_DIM,
            transcendentals=count,
        ),
        name="attend",
    )(me, block_map, x_own, squares, q_gain, *q_parts, *kv_parts)


def body(activations, w_query, w_keyval, q_gain, k_gain, stream_ids, local_times, block_map):
    row_count = activations.shape[0]
    group_size = HEADS // KV_HEADS
    q_width = w_query.shape[2]
    q_local = q_width // HEAD_DIM
    per_group = min(group_size, q_local)
    kv_local = q_local // per_group
    replicas = max(1, lax.axis_size("head") // KV_HEADS)
    head_index = lax.axis_index("head")
    first_group = head_index * q_local // group_size
    size = lax.axis_size("seq")
    far = size // NEAR
    me = lax.axis_index("seq").reshape(1)

    info = jnp.pad(jnp.stack([stream_ids, local_times]), ((0, INFO - 2), (0, 0)))
    x_send = pack(activations, info, me, far)
    x_parts = [x_send[0]] + [swap(x_send[k], k * NEAR) for k in range(1, far)]

    groups = [[f * NEAR + j for j in range(NEAR)] for f in range(far)]

    def near_weights(w):
        return lax.all_gather(w, "seq", axis=1, tiled=True, axis_index_groups=groups)

    kv_weights = lax.dynamic_slice_in_dim(
        w_keyval, first_group * (2 * HEAD_DIM), kv_local * 2 * HEAD_DIM, 2
    )
    q_chunks = 2 if q_width % 512 == 0 else 1
    chunk = q_width // q_chunks

    def partial_sums(w):
        parts = project(x_parts, near_weights(w))
        return [parts[0]] + [swap(parts[k], k * NEAR) for k in range(1, far)]

    kv_total, key_sq = reduce([partial_sums(kv_weights)], HEAD_DIM)
    key_sq = head_sum(jnp.where(head_index % replicas == 0, key_sq, jnp.float32(0.0)))
    kv_gain = lax.dynamic_slice_in_dim(k_gain, first_group * HEAD_DIM, kv_local * HEAD_DIM, 1)
    kv_rows = normalize(kv_total, key_sq, kv_gain, x_parts[0])
    times = jnp.stack([part[row_count + 1, :row_count] for part in x_parts])
    times = times.reshape(-1, kv_rows.shape[1])
    times = jnp.pad(times, ((0, -times.shape[0] % 16), (0, 0)))
    kv_here = jnp.concatenate(
        [kv_rows] + [swap(kv_rows, k * NEAR) for k in range(1, far)] + [times]
    )
    kv_other = swap(kv_here, 2)
    kv_parts = [kv_here, swap(kv_here, 1), kv_other, swap(kv_other, 1)]

    q_parts = [partial_sums(w_query[:, :, c * chunk:(c + 1) * chunk]) for c in range(q_chunks)]
    *q_totals, query_sq = reduce(q_parts, 2 * HEAD_DIM)
    query_sq = head_sum(query_sq)
    return attend(
        me, block_map, x_parts[0], query_sq, q_gain, q_totals, kv_parts, far, kv_local, per_group
    )


def solution(mesh):
    placed = (
        P("seq", None),
        P(None, "seq", "head"),
        P(None, "seq", None),
        P(None, "head"),
        P(),
        P("seq"),
        P("seq"),
        P(),
    )
    return jax.shard_map(
        body, mesh=mesh, in_specs=placed, out_specs=P("seq", "head"), check_vma=False
    )
```

```python
import functools
import math

import jax
import jax.numpy as jnp
from jax import lax
from jax.experimental import pallas as pl
from jax.experimental.pallas import tpu as pltpu
from jax.sharding import PartitionSpec as P

HEADS = 16
KV_HEADS = 4
HEAD_DIM = 128
STREAMS = 3
FRAMES = 32
NEAR = 4
INFO = 8

epsilon = 1e-06
MIB = 1024 * 1024

VMEM = pl.BlockSpec(memory_space=pltpu.VMEM)
SMEM = pl.BlockSpec(memory_space=pltpu.SMEM)


def params(mib):
    return pltpu.CompilerParams(vmem_limit_bytes=mib * MIB)


def swap(x, mask):
    size = lax.axis_size("seq")
    return lax.ppermute(x, "seq", [(i, i ^ mask) for i in range(size)])


def after(x, *others):
    return lax.optimization_barrier((x,) + others)[0]


def head_sum(x):
    size = lax.axis_size("head")
    step = 1
    while step < size:
        x = x + lax.ppermute(x, "head", [(i, i ^ step) for i in range(size)])
        step *= 2
    return x


def to_row(column):
    return jnp.broadcast_to(column, (column.shape[0], 128)).T[:8]


def to_column(row):
    return jnp.broadcast_to(row, (128, row.shape[1])).T[:, :1]


def by_stream(ids, gain_ref, first, width):
    gain = jnp.zeros((ids.shape[0], width), jnp.float32)
    for s in range(STREAMS):
        gain = jnp.where(ids == s, gain_ref[s:s + 1, first:first + width], gain)
    return gain


def pack_kernel(far, me_ref, x_ref, info_ref, out_ref):
    rows = x_ref.shape[0]
    depth = x_ref.shape[1] // (far * NEAR)
    near = me_ref[0] % NEAR
    info = info_ref[...].astype(jnp.bfloat16)
    for k in range(far):
        for j in range(NEAR):
            source = (k * NEAR + (near ^ j)) * depth
            if depth % 128 == 0:
                piece = x_ref[:, pl.ds(pl.multiple_of(source, 128), depth)]
            else:
                lane = source % 128
                wide = x_ref[:, pl.ds(pl.multiple_of(source - lane, 128), 128)]
                piece = wide[:, :depth]
                for first in range(depth, 128, depth):
                    piece = jnp.where(lane == first, wide[:, first:first + depth], piece)
            out_ref[k, :rows, j * depth:(j + 1) * depth] = piece
        out_ref[k, rows:, :rows] = info


def pack(x, info, me, far):
    rows, width = x.shape
    return pl.pallas_call(
        functools.partial(pack_kernel, far),
        out_shape=jax.ShapeDtypeStruct((far, rows + INFO, width // far), x.dtype),
        in_specs=[SMEM, VMEM, VMEM],
        out_specs=VMEM,
        compiler_params=params(16),
        cost_estimate=pl.CostEstimate(flops=0, bytes_accessed=4 * rows * width, transcendentals=0),
        name="pack",
    )(me, x, info)


def project_kernel(far, rows, *refs):
    w_refs, x_ref, out_ref = refs[:NEAR], refs[NEAR], refs[NEAR + 1]
    streams, depth, tile = w_refs[0].shape
    x = jnp.concatenate([x_ref[k, :rows] for k in range(far)], axis=0)
    ids = jnp.concatenate(
        [to_column(x_ref[k, rows:rows + 1, :rows].astype(jnp.float32)) for k in range(far)], axis=0
    )
    total = None
    for j in range(NEAR):
        part = x[:, j * depth:(j + 1) * depth]
        chosen = [jnp.where(ids == s, part, jnp.zeros_like(part)) for s in range(STREAMS)]
        term = jnp.dot(
            jnp.concatenate(chosen, axis=1),
            w_refs[j][...].reshape(streams * depth, tile),
            preferred_element_type=jnp.float32,
        )
        total = term if total is None else total + term
    for k in range(far):
        out_ref[k] = total[k * rows:(k + 1) * rows].astype(jnp.bfloat16)


def project(x_all, w_parts, offsets, columns):
    far, padded, width = x_all.shape
    rows = padded - INFO
    streams, depth, _ = w_parts[0].shape
    tile = min(256, columns)
    return pl.pallas_call(
        functools.partial(project_kernel, far, rows),
        grid=(columns // tile,),
        out_shape=jax.ShapeDtypeStruct((far, rows, columns), jnp.bfloat16),
        in_specs=[
            pl.BlockSpec((streams, depth, tile), lambda i, start=start // tile: (0, 0, i + start))
            for start in offsets
        ]
        + [pl.BlockSpec((far, padded, width), lambda i: (0, 0, 0))],
        out_specs=pl.BlockSpec((far, rows, tile), lambda i: (0, 0, i)),
        compiler_params=params(24),
        cost_estimate=pl.CostEstimate(
            flops=2 * far * rows * width * streams * columns,
            bytes_accessed=2 * (far * rows * (width + columns) + NEAR * streams * depth * columns),
            transcendentals=0,
        ),
        name="project",
    )(*w_parts, x_all)


def reduce_kernel(square_columns, *refs):
    half = len(refs) // 2
    squares = None
    for parts_ref, total_ref in zip(refs[:half], refs[half:-1]):
        total = parts_ref[0].astype(jnp.float32)
        for k in range(1, parts_ref.shape[0]):
            total = total + parts_ref[k].astype(jnp.float32)
        total_ref[...] = total
        for first in range(0, total.shape[1], 2 * HEAD_DIM):
            block = total[:, first:first + square_columns]
            term = jnp.sum(block * block, axis=1, keepdims=True)
            squares = term if squares is None else squares + term
    refs[-1][...] = to_row(squares)


def reduce(parts, square_columns):
    far, rows, columns = parts[0].shape
    return pl.pallas_call(
        functools.partial(reduce_kernel, square_columns),
        out_shape=[jax.ShapeDtypeStruct((rows, columns), jnp.float32)] * len(parts)
        + [jax.ShapeDtypeStruct((8, rows), jnp.float32)],
        in_specs=[VMEM] * len(parts),
        out_specs=[VMEM] * (len(parts) + 1),
        compiler_params=params(16),
        cost_estimate=pl.CostEstimate(
            flops=2 * len(parts) * far * rows * columns,
            bytes_accessed=3 * len(parts) * far * rows * columns,
            transcendentals=0,
        ),
        name="reduce",
    )(*parts)


def normalize_kernel(total_ref, square_ref, gain_ref, info_ref, out_ref):
    ids = to_column(info_ref[:1].astype(jnp.float32))
    scale = to_column(lax.rsqrt(square_ref[:1] / (KV_HEADS * HEAD_DIM) + epsilon))
    for g in range(gain_ref.shape[1] // HEAD_DIM):
        first = 2 * g * HEAD_DIM
        gain = by_stream(ids, gain_ref, g * HEAD_DIM, HEAD_DIM)
        key = total_ref[:, first:first + HEAD_DIM] * scale * gain
        out_ref[:, first:first + HEAD_DIM] = key.astype(jnp.bfloat16)
        value = total_ref[:, first + HEAD_DIM:first + 2 * HEAD_DIM]
        out_ref[:, first + HEAD_DIM:first + 2 * HEAD_DIM] = value.astype(jnp.bfloat16)


def normalize(total, squares, gain, info):
    return pl.pallas_call(
        normalize_kernel,
        out_shape=jax.ShapeDtypeStruct(total.shape, jnp.bfloat16),
        in_specs=[VMEM] * 4,
        out_specs=VMEM,
        compiler_params=params(16),
        cost_estimate=pl.CostEstimate(
            flops=4 * total.size, bytes_accessed=6 * total.size, transcendentals=0
        ),
        name="normalize",
    )(total, squares, gain, info)


def attend_kernel(kv_local, per_group, q_count, far, me_ref, map_ref, info_ref, square_ref, gain_ref,
                  *refs):
    q_refs, kv_refs = refs[:q_count], refs[q_count:q_count + NEAR]
    out_ref, score_ref = refs[-2:]
    rows, columns = q_refs[0].shape
    keys = far * rows
    kv_columns = kv_refs[0].shape[1]
    exponent = math.log2(math.e) / math.sqrt(HEAD_DIM)
    near = me_ref[0] % NEAR
    first_half = lax.broadcasted_iota(jnp.int32, (1, rows), 1) < rows // 2
    ids = to_column(info_ref[:1].astype(jnp.float32))
    q_scale = to_column(lax.rsqrt(square_ref[:1] / (HEADS * HEAD_DIM) + epsilon))

    key_times = []
    for j in range(NEAR):
        pieces = []
        for k in range(far):
            owner = k * NEAR + (near ^ j)
            row, lane = divmod(k * rows, kv_columns)
            local = kv_refs[j][keys + row:keys + row + 1, lane:lane + rows].astype(jnp.float32)
            block = jnp.where(first_half, map_ref[2 * owner], map_ref[2 * owner + 1])
            pieces.append((block * FRAMES).astype(jnp.float32) + local)
        key_times.append(jnp.concatenate(pieces, axis=1))
    local = info_ref[1:2].astype(jnp.float32)
    block = jnp.where(first_half, map_ref[2 * me_ref[0]], map_ref[2 * me_ref[0] + 1])
    query_times = to_column((block * FRAMES).astype(jnp.float32) + local)

    query_times = jnp.concatenate([query_times] * per_group, axis=0)
    for g in range(kv_local):
        queries = []
        for h in range(per_group):
            head = g * per_group + h
            chunk, first = divmod(head * HEAD_DIM, columns)
            gain = by_stream(ids, gain_ref, head * HEAD_DIM, HEAD_DIM)
            queries.append(q_refs[chunk][:, first:first + HEAD_DIM] * q_scale * gain)
        q = jnp.concatenate(queries, axis=0).astype(jnp.bfloat16)
        peak = None
        for j in range(NEAR):
            key = kv_refs[j][:keys, 2 * g * HEAD_DIM:(2 * g + 1) * HEAD_DIM]
            score = lax.dot_general(
                q, key, (((1,), (1,)), ((), ())), preferred_element_type=jnp.float32
            )
            score = jnp.where(key_times[j] <= query_times, score, -1e30)
            score_ref[j] = score
            top = jnp.max(score, axis=1, keepdims=True)
            peak = top if peak is None else jnp.maximum(peak, top)
        total = jnp.zeros((per_group * rows, 1), jnp.float32)
        mixed = jnp.zeros((per_group * rows, HEAD_DIM), jnp.float32)
        for j in range(NEAR):
            value = kv_refs[j][:keys, (2 * g + 1) * HEAD_DIM:(2 * g + 2) * HEAD_DIM]
            terms = jnp.exp2((score_ref[j] - peak) * exponent)
            total = total + jnp.sum(terms, axis=1, keepdims=True)
            mixed = mixed + jnp.dot(
                terms.astype(jnp.bfloat16), value, preferred_element_type=jnp.float32
            )
        out = (mixed / total).astype(out_ref.dtype)
        for h in range(per_group):
            first = (g * per_group + h) * HEAD_DIM
            out_ref[:, first:first + HEAD_DIM] = out[h * rows:(h + 1) * rows]


def attend(me, block_map, info, squares, q_gain, q_parts, kv_parts, far, kv_local, per_group):
    rows, columns = q_parts[0].shape
    keys = NEAR * far * rows
    count = rows * kv_local * per_group * keys
    return pl.pallas_call(
        functools.partial(attend_kernel, kv_local, per_group, len(q_parts), far),
        out_shape=jax.ShapeDtypeStruct((rows, columns * len(q_parts)), jnp.bfloat16),
        in_specs=[SMEM, SMEM] + [VMEM] * (3 + len(q_parts) + NEAR),
        out_specs=VMEM,
        scratch_shapes=[pltpu.VMEM((NEAR, per_group * rows, far * rows), jnp.float32)],
        compiler_params=params(40),
        cost_estimate=pl.CostEstimate(
            flops=4 * count * HEAD_DIM,
            bytes_accessed=4 * keys * kv_local * HEAD_DIM,
            transcendentals=count,
        ),
        name="attend",
    )(me, block_map, info, squares, q_gain, *q_parts, *kv_parts)


def body(activations, w_query, w_keyval, q_gain, k_gain, stream_ids, local_times, block_map):
    row_count = activations.shape[0]
    group_size = HEADS // KV_HEADS
    q_width = w_query.shape[2]
    q_local = q_width // HEAD_DIM
    per_group = min(group_size, q_local)
    kv_local = q_local // per_group
    replicas = max(1, lax.axis_size("head") // KV_HEADS)
    head_index = lax.axis_index("head")
    first_group = head_index * q_local // group_size
    size = lax.axis_size("seq")
    far = size // NEAR
    me = lax.axis_index("seq").reshape(1)

    info = jnp.pad(jnp.stack([stream_ids, local_times]), ((0, INFO - 2), (0, 0)))
    groups = [[f * NEAR + j for f in range(far)] for j in range(NEAR)]

    def exchange(parts):
        return lax.all_to_all(parts, "seq", 0, 0, axis_index_groups=groups)

    kv_width = kv_local * 2 * HEAD_DIM
    kv_weights = lax.dynamic_slice_in_dim(
        w_keyval, first_group * (2 * HEAD_DIM), kv_width, 2
    )
    q_chunks = 2 if q_width % 512 == 0 else 1
    chunk = q_width // q_chunks
    q_starts = range(0, q_width, chunk)
    q_weights = [w_query[:, :, start:start + chunk] for start in q_starts]

    packed = pack(activations, info, me, far)
    kv_other = swap(kv_weights, 2)
    q_others = [swap(after(q_weights[0], packed, kv_weights), 2)]
    x_all = exchange(packed)
    q_others += [swap(after(w, x_all, kv_other), 2) for w in q_weights[1:]]
    kv_core = swap(after(kv_weights, x_all), 1)
    q_core = swap(after(w_query, x_all), 1)

    def partial_sums(own, core, other, start, columns, gate):
        other_core = swap(after(other, gate), 1)
        return project(
            x_all, [own, core, other, other_core], [start, start, 0, 0], columns
        )

    gate = partial_sums(kv_weights, kv_core, kv_other, 0, kv_width, x_all)
    kv_total, key_sq = reduce([exchange(gate)], HEAD_DIM)
    key_sq = head_sum(jnp.where(head_index % replicas == 0, key_sq, jnp.float32(0.0)))
    kv_gain = lax.dynamic_slice_in_dim(k_gain, first_group * HEAD_DIM, kv_local * HEAD_DIM, 1)
    kv_rows = normalize(kv_total, key_sq, kv_gain, info)
    times = x_all[:, row_count + 1, :row_count].reshape(-1, kv_rows.shape[1])
    times = jnp.pad(times, ((0, -times.shape[0] % 16), (0, 0)))
    kv_here = exchange(jnp.broadcast_to(kv_rows, (far,) + kv_rows.shape))
    kv_here = jnp.concatenate([kv_here.reshape(far * row_count, -1), times])
    kv_other = swap(kv_here, 2)
    kv_parts = [kv_here, swap(kv_here, 1), kv_other, swap(kv_other, 1)]

    q_parts = []
    for other, start in zip(q_others, q_starts):
        gate = partial_sums(w_query, q_core, other, start, chunk, gate)
        q_parts.append(exchange(gate))
    *q_totals, query_sq = reduce(q_parts, 2 * HEAD_DIM)
    query_sq = head_sum(query_sq)
    return attend(
        me, block_map, info, query_sq, q_gain, q_totals, kv_parts, far, kv_local, per_group
    )


def solution(mesh):
    placed = (
        P("seq", None),
        P(None, "seq", "head"),
        P(None, "seq", None),
        P(None, "head"),
        P(),
        P("seq"),
        P("seq"),
        P(),
    )
    return jax.shard_map(
        body, mesh=mesh, in_specs=placed, out_specs=P("seq", "head"), check_vma=False
    )
```

```python
import functools
import math

import jax
import jax.numpy as jnp
from jax import lax
from jax.experimental import pallas as pl
from jax.experimental.pallas import tpu as pltpu
from jax.sharding import PartitionSpec as P

HEADS = 16
KV_HEADS = 4
HEAD_DIM = 128
STREAMS = 3
FRAMES = 32
NEAR = 4
INFO = 8

epsilon = 1e-06
MIB = 1024 * 1024

VMEM = pl.BlockSpec(memory_space=pltpu.VMEM)
SMEM = pl.BlockSpec(memory_space=pltpu.SMEM)


def params(mib):
    return pltpu.CompilerParams(vmem_limit_bytes=mib * MIB)


def swap(x, mask):
    size = lax.axis_size("seq")
    return lax.ppermute(x, "seq", [(i, i ^ mask) for i in range(size)])


def head_swap(x):
    size = lax.axis_size("head")
    return lax.ppermute(x, "head", [(i, i ^ 1) for i in range(size)])


def after(x, *others):
    return lax.optimization_barrier((x,) + others)[0]


def head_sum(x):
    size = lax.axis_size("head")
    step = 1
    while step < size:
        x = x + lax.ppermute(x, "head", [(i, i ^ step) for i in range(size)])
        step *= 2
    return x


def to_row(column):
    return jnp.broadcast_to(column, (column.shape[0], 128)).T[:8]


def to_column(row):
    return jnp.broadcast_to(row, (128, row.shape[1])).T[:, :1]


def by_stream(ids, gain_ref, first, width):
    gain = jnp.zeros((ids.shape[0], width), jnp.float32)
    for s in range(STREAMS):
        gain = jnp.where(ids == s, gain_ref[s:s + 1, first:first + width], gain)
    return gain


def pack_kernel(far, me_ref, x_ref, info_ref, *out_refs):
    rows = x_ref.shape[0]
    depth = x_ref.shape[1] // (far * NEAR)
    me = me_ref[0]
    half = me_ref[1] * (NEAR // 2)
    info = info_ref[...].astype(jnp.bfloat16)
    for k in range(far):
        for j in range(NEAR if k == 0 else NEAR // 2):
            source = (me ^ (k * NEAR + (j if k == 0 else j + half))) * depth
            if depth % 128 == 0:
                piece = x_ref[:, pl.ds(pl.multiple_of(source, 128), depth)]
            else:
                lane = source % 128
                wide = x_ref[:, pl.ds(pl.multiple_of(source - lane, 128), 128)]
                piece = wide[:, :depth]
                for first in range(depth, 128, depth):
                    piece = jnp.where(lane == first, wide[:, first:first + depth], piece)
            out_refs[k][:rows, j * depth:(j + 1) * depth] = piece
        out_refs[k][rows:, :rows] = info


def pack(x, info, me, far):
    rows, width = x.shape
    width = width // far
    return pl.pallas_call(
        functools.partial(pack_kernel, far),
        out_shape=[jax.ShapeDtypeStruct((rows + INFO, width), x.dtype)]
        + [jax.ShapeDtypeStruct((rows + INFO, width // 2), x.dtype)] * (far - 1),
        in_specs=[SMEM, VMEM, VMEM],
        out_specs=[VMEM] * far,
        compiler_params=params(16),
        cost_estimate=pl.CostEstimate(flops=0, bytes_accessed=2 * x.size, transcendentals=0),
        name="pack",
    )(me, x, info)


def project_kernel(far, rows, me_ref, *refs):
    w_refs, x_refs = refs[:NEAR], refs[NEAR:NEAR + 2 * far - 1]
    out_refs, spread_ref = refs[NEAR + 2 * far - 1:-1], refs[-1]
    streams, depth, tile = w_refs[0].shape

    @pl.when(pl.program_id(0) == 0)
    def _():
        upper = me_ref[1] == 1
        for k in range(far):
            mine = x_refs[max(2 * k - 1, 0)]
            ids = to_column(mine[rows:rows + 1, :rows].astype(jnp.float32))
            for j in range(NEAR):
                if k == 0:
                    part = mine[:rows, j * depth:(j + 1) * depth]
                else:
                    first = j % (NEAR // 2) * depth
                    part = mine[:rows, first:first + depth]
                    theirs = x_refs[2 * k][:rows, first:first + depth]
                    part = jnp.where(upper == (j >= NEAR // 2), part, theirs)
                for s in range(streams):
                    first = (j * streams + s) * depth
                    spread_ref[k * rows:(k + 1) * rows, first:first + depth] = jnp.where(
                        ids == s, part, jnp.zeros_like(part)
                    )

    total = None
    for j in range(NEAR):
        term = jnp.dot(
            spread_ref[:, j * streams * depth:(j + 1) * streams * depth],
            w_refs[j][...].reshape(streams * depth, tile),
            preferred_element_type=jnp.float32,
        )
        total = term if total is None else total + term
    out_refs[0][...] = total[:rows]
    for k in range(1, far):
        out_refs[k][...] = total[k * rows:(k + 1) * rows].astype(jnp.bfloat16)


def project(me, x_parts, w_parts, offsets, columns):
    far = (len(x_parts) + 1) // 2
    padded, width = x_parts[0].shape
    rows = padded - INFO
    streams, depth, _ = w_parts[0].shape
    tile = min(256, columns)
    shapes = [jax.ShapeDtypeStruct((rows, columns), jnp.float32)]
    shapes += [jax.ShapeDtypeStruct((rows, columns), jnp.bfloat16)] * (far - 1)
    return pl.pallas_call(
        functools.partial(project_kernel, far, rows),
        grid=(columns // tile,),
        out_shape=shapes,
        in_specs=[SMEM]
        + [
            pl.BlockSpec((streams, depth, tile), lambda i, start=start // tile: (0, 0, i + start))
            for start in offsets
        ]
        + [pl.BlockSpec(part.shape, lambda i: (0, 0)) for part in x_parts],
        out_specs=[pl.BlockSpec((rows, tile), lambda i: (0, i))] * far,
        scratch_shapes=[pltpu.VMEM((far * rows, streams * width), jnp.bfloat16)],
        compiler_params=params(24),
        cost_estimate=pl.CostEstimate(
            flops=2 * far * rows * width * streams * columns,
            bytes_accessed=2 * (far * rows * (width + columns) + NEAR * streams * depth * columns),
            transcendentals=0,
        ),
        name="project",
    )(me, *w_parts, *x_parts)


def reduce_kernel(far, square_columns, *refs):
    part_refs, total_ref, square_ref = refs[:-2], refs[-2], refs[-1]
    squares = None
    start = 0
    for own_ref, *other_refs in (part_refs[c:c + far] for c in range(0, len(part_refs), far)):
        total = own_ref[...]
        for ref in other_refs:
            total = total + ref[...].astype(jnp.float32)
        total_ref[:, start:start + total.shape[1]] = total
        start += total.shape[1]
        for first in range(0, total.shape[1], 2 * HEAD_DIM):
            block = total[:, first:first + square_columns]
            term = jnp.sum(block * block, axis=1, keepdims=True)
            squares = term if squares is None else squares + term
    square_ref[...] = to_row(squares)


def reduce(part_lists, square_columns):
    rows = part_lists[0][0].shape[0]
    columns = sum(parts[0].shape[1] for parts in part_lists)
    far = len(part_lists[0])
    parts = [part for parts in part_lists for part in parts]
    return pl.pallas_call(
        functools.partial(reduce_kernel, far, square_columns),
        out_shape=[
            jax.ShapeDtypeStruct((rows, columns), jnp.float32),
            jax.ShapeDtypeStruct((8, rows), jnp.float32),
        ],
        in_specs=[VMEM] * len(parts),
        out_specs=[VMEM] * 2,
        compiler_params=params(16),
        cost_estimate=pl.CostEstimate(
            flops=2 * far * rows * columns, bytes_accessed=3 * far * rows * columns,
            transcendentals=0,
        ),
        name="reduce",
    )(*parts)


def normalize_kernel(total_ref, square_ref, gain_ref, x_ref, out_ref):
    rows = total_ref.shape[0]
    ids = to_column(x_ref[rows:rows + 1, :rows].astype(jnp.float32))
    scale = to_column(lax.rsqrt(square_ref[:1] / (KV_HEADS * HEAD_DIM) + epsilon))
    for g in range(gain_ref.shape[1] // HEAD_DIM):
        first = 2 * g * HEAD_DIM
        gain = by_stream(ids, gain_ref, g * HEAD_DIM, HEAD_DIM)
        key = total_ref[:, first:first + HEAD_DIM] * scale * gain
        out_ref[:, first:first + HEAD_DIM] = key.astype(jnp.bfloat16)
        value = total_ref[:, first + HEAD_DIM:first + 2 * HEAD_DIM]
        out_ref[:, first + HEAD_DIM:first + 2 * HEAD_DIM] = value.astype(jnp.bfloat16)


def normalize(total, squares, gain, x_own):
    return pl.pallas_call(
        normalize_kernel,
        out_shape=jax.ShapeDtypeStruct(total.shape, jnp.bfloat16),
        in_specs=[VMEM] * 4,
        out_specs=VMEM,
        compiler_params=params(16),
        cost_estimate=pl.CostEstimate(
            flops=4 * total.size, bytes_accessed=6 * total.size, transcendentals=0
        ),
        name="normalize",
    )(total, squares, gain, x_own)


def attend_kernel(kv_local, per_group, far, me_ref, map_ref, x_ref, square_ref, gain_ref, q_ref,
                  *refs):
    kv_refs, out_ref, score_ref = refs[:NEAR], refs[-2], refs[-1]
    rows = q_ref.shape[0]
    keys = far * rows
    kv_columns = kv_refs[0].shape[1]
    exponent = math.log2(math.e) / math.sqrt(HEAD_DIM)
    me = me_ref[0]
    first_half = lax.broadcasted_iota(jnp.int32, (1, rows), 1) < rows // 2
    ids = to_column(x_ref[rows:rows + 1, :rows].astype(jnp.float32))
    q_scale = to_column(lax.rsqrt(square_ref[:1] / (HEADS * HEAD_DIM) + epsilon))

    key_times = []
    for j in range(NEAR):
        pieces = []
        for k in range(far):
            owner = me ^ (k * NEAR + j)
            row, lane = divmod(k * rows, kv_columns)
            local = kv_refs[j][keys + row:keys + row + 1, lane:lane + rows].astype(jnp.float32)
            block = jnp.where(first_half, map_ref[2 * owner], map_ref[2 * owner + 1])
            pieces.append((block * FRAMES).astype(jnp.float32) + local)
        key_times.append(jnp.concatenate(pieces, axis=1))
    query_times = to_column(key_times[0][:, :rows])

    query_times = jnp.concatenate([query_times] * per_group, axis=0)
    for g in range(kv_local):
        queries = []
        for h in range(per_group):
            first = (g * per_group + h) * HEAD_DIM
            gain = by_stream(ids, gain_ref, first, HEAD_DIM)
            queries.append(q_ref[:, first:first + HEAD_DIM] * q_scale * gain)
        q = jnp.concatenate(queries, axis=0).astype(jnp.bfloat16)
        peak = None
        for j in range(NEAR):
            key = kv_refs[j][:keys, 2 * g * HEAD_DIM:(2 * g + 1) * HEAD_DIM]
            score = lax.dot_general(
                q, key, (((1,), (1,)), ((), ())), preferred_element_type=jnp.float32
            )
            score = jnp.where(key_times[j] <= query_times, score, -1e30)
            score_ref[j] = score
            top = jnp.max(score, axis=1, keepdims=True)
            peak = top if peak is None else jnp.maximum(peak, top)
        total = jnp.zeros((per_group * rows, 1), jnp.float32)
        mixed = jnp.zeros((per_group * rows, HEAD_DIM), jnp.float32)
        for j in range(NEAR):
            value = kv_refs[j][:keys, (2 * g + 1) * HEAD_DIM:(2 * g + 2) * HEAD_DIM]
            terms = jnp.exp2((score_ref[j] - peak) * exponent)
            total = total + jnp.sum(terms, axis=1, keepdims=True)
            mixed = mixed + jnp.dot(
                terms.astype(jnp.bfloat16), value, preferred_element_type=jnp.float32
            )
        out = (mixed / total).astype(out_ref.dtype)
        for h in range(per_group):
            first = (g * per_group + h) * HEAD_DIM
            out_ref[:, first:first + HEAD_DIM] = out[h * rows:(h + 1) * rows]


def attend(me, block_map, x_own, squares, q_gain, q, kv_parts, far, kv_local, per_group):
    rows = q.shape[0]
    keys = NEAR * far * rows
    count = rows * kv_local * per_group * keys
    return pl.pallas_call(
        functools.partial(attend_kernel, kv_local, per_group, far),
        out_shape=jax.ShapeDtypeStruct(q.shape, jnp.bfloat16),
        in_specs=[SMEM, SMEM] + [VMEM] * (4 + NEAR),
        out_specs=VMEM,
        scratch_shapes=[pltpu.VMEM((NEAR, per_group * rows, far * rows), jnp.float32)],
        compiler_params=params(40),
        cost_estimate=pl.CostEstimate(
            flops=4 * count * HEAD_DIM,
            bytes_accessed=4 * keys * kv_local * HEAD_DIM,
            transcendentals=count,
        ),
        name="attend",
    )(me, block_map, x_own, squares, q_gain, q, *kv_parts)


def body(activations, w_query, w_keyval, q_gain, k_gain, stream_ids, local_times, block_map):
    row_count = activations.shape[0]
    group_size = HEADS // KV_HEADS
    q_width = w_query.shape[2]
    q_local = q_width // HEAD_DIM
    per_group = min(group_size, q_local)
    kv_local = q_local // per_group
    replicas = max(1, lax.axis_size("head") // KV_HEADS)
    head_index = lax.axis_index("head")
    first_group = head_index * q_local // group_size
    size = lax.axis_size("seq")
    far = size // NEAR
    me = jnp.stack([lax.axis_index("seq"), head_index % 2])

    info = jnp.pad(jnp.stack([stream_ids, local_times]), ((0, INFO - 2), (0, 0)))
    packed = pack(activations, info, me, far)
    halves = [swap(packed[k], k * NEAR) for k in range(1, far)]
    x_parts = [packed[0]]
    for half in halves:
        x_parts += [half, head_swap(half)]

    kv_width = kv_local * 2 * HEAD_DIM
    kv_weights = lax.dynamic_slice_in_dim(
        w_keyval, first_group * (2 * HEAD_DIM), kv_width, 2
    )
    tiles = max(1, q_width // 256)
    q_widths = [width * q_width // tiles for width in (tiles - tiles // 2, tiles // 2) if width]
    q_starts = [sum(q_widths[:c]) for c in range(len(q_widths))]
    q_weights = [
        w_query[:, :, start:start + width] for start, width in zip(q_starts, q_widths)
    ]
    kv_other = swap(kv_weights, 2)
    q_others = [swap(q_weights[0], 2)]
    q_others += [swap(after(w, q_others[0]), 2) for w in q_weights[1:]]
    kv_core = swap(after(kv_weights, *x_parts), 1)

    def partial_sums(own, core, other, start, gate):
        other_core = swap(after(other, *gate), 1)
        parts = project(
            me, x_parts, [own, core, other, other_core], [start, start, 0, 0], other.shape[2]
        )
        return [parts[0]] + [swap(parts[k], k * NEAR) for k in range(1, far)], parts

    kv_parts, gate = partial_sums(kv_weights, kv_core, kv_other, 0, x_parts)
    q_core = swap(after(w_query, *gate), 1)
    kv_total, key_sq = reduce([kv_parts], HEAD_DIM)
    key_sq = head_sum(jnp.where(head_index % replicas == 0, key_sq, jnp.float32(0.0)))
    kv_gain = lax.dynamic_slice_in_dim(k_gain, first_group * HEAD_DIM, kv_local * HEAD_DIM, 1)
    kv_rows = normalize(kv_total, key_sq, kv_gain, x_parts[0])
    times = jnp.stack([part[row_count + 1, :row_count] for part in [packed[0]] + halves])
    times = times.reshape(-1, kv_rows.shape[1])
    times = jnp.pad(times, ((0, -times.shape[0] % 16), (0, 0)))
    kv_here = jnp.concatenate(
        [kv_rows] + [swap(kv_rows, k * NEAR) for k in range(1, far)] + [times]
    )
    q_parts, gate = [], [kv_total]
    for other, start in zip(q_others, q_starts):
        parts, sent = partial_sums(w_query, q_core, other, start, gate)
        q_parts.append(parts)
        if start == 0:
            kv_here = after(kv_here, *sent)
            kv_other = swap(kv_here, 2)
            gate = [kv_here]
            kv_core = swap(after(kv_here, *parts), 1)
            kv_parts = [kv_here, kv_core, kv_other, swap(after(kv_other, *parts), 1)]

    queries, query_sq = reduce(q_parts, 2 * HEAD_DIM)
    query_sq = head_sum(query_sq)
    return attend(
        me, block_map, x_parts[0], query_sq, q_gain, queries, kv_parts, far, kv_local, per_group
    )


def solution(mesh):
    placed = (
        P("seq", None),
        P(None, "seq", "head"),
        P(None, "seq", None),
        P(None, "head"),
        P(),
        P("seq"),
        P("seq"),
        P(),
    )
    return jax.shard_map(
        body, mesh=mesh, in_specs=placed, out_specs=P("seq", "head"), check_vma=False
    )
```
